32 devices in a mesh: seq: 16 (over z, y, x), tp: 2 (over core).
Axes of the slice: x: 2, y: 2, z: 4, core: 2. Of those that a mesh axis runs over, the one named last changes fastest.
Arguments:
- tokens: bfloat16 [2048, 2048], P(('seq', 'tp')), may hold values from -6 to 6
- block_ids: int32 [16, 2], replicated, may hold values from 0 to 31, as said below
- attn_gain: float32 [2048], replicated, may hold values from 0.25 to 1.75
- q_weight: bfloat16 [2048, 3072], P(None, 'tp'), may hold values from -0.125 to 0.125
- kv_weight: bfloat16 [2048, 576], replicated, may hold values from -0.125 to 0.125
- kv_gain: float32 [512], replicated, may hold values from 0.25 to 1.75
- uk_weight: bfloat16 [16, 512, 128], P('tp'), may hold values from -40 to 40
- uv_weight: bfloat16 [16, 512, 128], P('tp'), may hold values from -0.25 to 0.25
- o_weight: bfloat16 [2048, 2048], P('tp'), may hold values from -0.125 to 0.125
- ffn_gain: float32 [2048], replicated, may hold values from 0.25 to 1.75
- w_gate: bfloat16 [16, 2048, 1408], P('seq', None, 'tp'), may hold values from -0.125 to 0.125
- w_up: bfloat16 [16, 2048, 1408], P('seq', None, 'tp'), may hold values from -0.125 to 0.125
- w_down: bfloat16 [16, 1408, 2048], P('seq', 'tp'), may hold values from -0.15625 to 0.15625
- routes: int32 [2048, 6], P('seq'), may hold values from 0 to 15, all different within a row; in each aligned block of 64 rows (0 to 63, 64 to 127, ...) at most 36 rows name the same one
- gate_weights: float32 [2048, 6], P('seq'), may hold values from 0.1 to 1
Outputs:
- layer_out: bfloat16 [2048, 2048], P(('seq', 'tp'))
The draws below stay inside these ranges and needn't reach their ends.
Inputs may be any that keep to these rules, and one draw needn't show every extreme that they name: `block_ids`: row d is (b, 31 - b) with b below 16; the first column names every b once. `routes`: each row names 6 different experts. In each aligned block of 64 rows (the tokens of one device) no expert is named by more than 36 rows, a bound that some block reaches.
All inputs are finite; a program needn't handle non-finite values.
Results may differ from the reference program's by a relative error of at most 0.027.
The reference program's roundings to bfloat16 on the way count: a program that leaves them out, or rounds other values in their place, can miss the bound.
Values may be sent and summed in bfloat16 or wider, within the bound.
No kernel may reach another device: no remote copies, remote signals or barrier semaphores. Data moves between devices by JAX's collectives and lax.ppermute only.
A program may use at most 128 MiB of HBM per device.

```python
import math
import jax
import jax.numpy as jnp
import numpy as np
from jax import lax

D = 2048
HEADS = 16
NOPE = 128
ROPE = 64
LATENT = 512
VDIM = 128
FFE = 1408
TOPK = 6
TOK_DEV = 128
EXPERTS = 16
TOKENS = 2048
SUB = 64
CAP = 36
N_SEQ = 16
DEVICES = 32


def draw_block_ids(key, part):
    lower = jax.random.permutation(key, N_SEQ).astype(jnp.int32)
    return jnp.stack([lower, 2 * N_SEQ - 1 - lower], axis=1)


def draw_uk_weight(key, part):
    base_key = jax.random.fold_in(key, 7301)
    normal_key = jax.random.fold_in(base_key, 0)
    values = jnp.clip(jax.random.normal(normal_key, (HEADS, LATENT, NOPE), jnp.float32), -6.0, 6.0) * LATENT ** (-0.5)
    return values.astype(jnp.bfloat16)


def block_levels(own_key, extent, cuts, low, largest):
    def one(dim, parts):
        steps = jax.random.uniform(jax.random.fold_in(jax.random.fold_in(own_key, 6), dim), (parts,), jnp.float32, low / len(cuts), largest / len(cuts))
        return jnp.repeat(jnp.exp(steps), extent[dim] // parts).reshape((-1,) + (1,) * (len(extent) - dim - 1))

    gain = one(*cuts[0])
    for cut in cuts[1:]:
        gain = gain * one(*cut)
    return gain


def deal_out(own_key, own, number, rows, amount, top, most, lean):
    sequence = jax.random.permutation(own_key, amount)
    heavy_load, usual = load_shares(amount, rows * top, most, lean, True), load_shares(amount, rows * top, most, lean, False)
    places = jnp.arange(amount)

    def named(sizes, turn):
        used = int((sizes > 0).sum())
        fixed = max(1, used // 4)
        passed = fixed + (places - fixed + turn * (used - fixed)) % max(1, amount - fixed)
        return jnp.zeros((amount,), jnp.int32).at[sequence[jnp.where(places < fixed, places, passed)]].set(jnp.asarray(sizes, jnp.int32))

    sizes = jnp.where(number % 4 == 0, named(heavy_load, number // 4), named(usual, number - number // 4 - 1))
    mixed = jax.random.permutation(jax.random.fold_in(own, 3), amount)
    source_of, receiver = mixed[0:amount // 2 * 2:2], mixed[1:amount // 2 * 2:2]
    room = jnp.minimum(sizes[source_of] - 1, most - sizes[receiver]) // 2
    room = jnp.where((source_of == sequence[0]) | (receiver == sequence[0]) | (sizes[receiver] == 0), 0, jnp.maximum(room, 0))
    passed = jax.random.randint(jax.random.fold_in(own, 4), (amount // 2,), 0, 1 << 20) % (room + 1)
    sizes = sizes.at[source_of].add(-passed).at[receiver].add(passed)
    members = jnp.searchsorted(jnp.cumsum(sizes), jnp.arange(rows * top), side="right").astype(jnp.int32)
    grid = members.reshape(top, rows).T
    grid = grid[jax.random.permutation(jax.random.fold_in(own, 1), rows)]
    turn = jax.random.randint(jax.random.fold_in(own, 2), (rows, 1), 0, top)
    return jnp.take_along_axis(grid, (jnp.arange(top)[None, :] + turn) % top, axis=1)


def load_shares(count, total, bound, skew, full):
    loads = [(1 << 20) // math.isqrt(rank ** skew) + 1 for rank in range(1, count + 1)]
    largest = bound if full else min(bound, max(-(-total // count), total * loads[0] // sum(loads)))
    least = 1 if total - largest >= count - 1 else 0
    given, spare = [largest] + [least] * (count - 1), total - largest - least * (count - 1)
    while spare > 0:
        free = [i for i in range(1, count) if given[i] < largest] or [i for i in range(1, count) if given[i] < bound]
        whole, left = sum([loads[i] for i in free]), spare
        for i in free:
            extra = min(bound - given[i], max(1, left * loads[i] // whole), spare)
            given[i] = given[i] + extra
            spare = spare - extra
    return np.array(given)


def bell_draw(own_key, extent, width, most, cuts=(), kind=jnp.bfloat16):
    array = width * jax.random.normal(own_key, extent, jnp.float32)
    if cuts:
        array = array * block_levels(own_key, extent, cuts, -0.22, 0.18)
    return jnp.clip(array, -most, most).astype(kind)


def setup_inputs(seed: int = 0) -> dict:
    streams_of = jax.random.split(jax.random.key(seed), 16)
    tokens = bell_draw(streams_of[0], (TOKENS, D), 1.0, 6.0, ((0, 32),))
    block_ids = draw_block_ids(jax.random.fold_in(streams_of[15], 71), 0)
    attn_gain = jnp.clip(1.0 + 0.15 * jax.random.normal(streams_of[2], (D,), jnp.float32), 0.25, 1.75)
    q_weight = bell_draw(streams_of[3], (D, HEADS * (NOPE + ROPE)), D ** -0.5, 0.125, ((1, 2),))
    kv_weight = bell_draw(streams_of[4], (D, LATENT + ROPE), D ** -0.5, 0.125)
    kv_gain = jnp.clip(1.0 + 0.15 * jax.random.normal(streams_of[5], (LATENT,), jnp.float32), 0.25, 1.75)
    uk_weight = draw_uk_weight(jax.random.fold_in(streams_of[15], 71), 0)
    uv_weight = bell_draw(streams_of[7], (HEADS, LATENT, VDIM), LATENT ** -0.5, 0.25, ((0, 2),))
    o_weight = bell_draw(streams_of[8], (HEADS * VDIM, D), (HEADS * VDIM) ** -0.5, 0.125, ((0, 2),))
    ffn_gain = jnp.clip(1.0 + 0.15 * jax.random.normal(streams_of[9], (D,), jnp.float32), 0.25, 1.75)
    w_gate = bell_draw(streams_of[10], (EXPERTS, D, FFE), D ** -0.5, 0.125, ((0, 16), (2, 2)))
    w_up = bell_draw(streams_of[11], (EXPERTS, D, FFE), D ** -0.5, 0.125, ((0, 16), (2, 2)))
    w_down = bell_draw(streams_of[12], (EXPERTS, FFE, D), FFE ** -0.5, 0.15625, ((0, 16), (1, 2)))
    routes_keys = jax.random.split(jax.random.fold_in(streams_of[13], 1), TOKENS // SUB)
    routes_turns = jax.random.permutation(jax.random.fold_in(streams_of[13], 3), TOKENS // SUB)
    routes = jax.vmap(lambda own, number: deal_out(jax.random.fold_in(streams_of[13], 2), own, number, SUB, EXPERTS, TOPK, CAP, 2))(routes_keys, routes_turns).reshape((TOKENS, TOPK))
    gate_weights = jnp.clip(jnp.exp(math.log(1.0) - 2.3025851 * jax.random.uniform(streams_of[14], (TOKENS, TOPK), jnp.float32) ** block_levels(streams_of[14], (TOKENS, TOPK), ((0, 16),), -0.2, 0.2)), 0.1, 1.0)
    return {"tokens": tokens, "block_ids": block_ids, "attn_gain": attn_gain, "q_weight": q_weight, "kv_weight": kv_weight, "kv_gain": kv_gain, "uk_weight": uk_weight, "uv_weight": uv_weight, "o_weight": o_weight, "ffn_gain": ffn_gain, "w_gate": w_gate, "w_up": w_up, "w_down": w_down, "routes": routes, "gate_weights": gate_weights}


EPSILON = 1e-06

def normalize(values, gain_vec):
    values = values.astype(jnp.float32)
    factor = lax.rsqrt(lax.optimization_barrier(jnp.mean(values * values, axis=-1, keepdims=True)) + EPSILON)
    return values * factor * gain_vec

def rotate(values, position):
    half_width = values.shape[-1] // 2
    frequency = jnp.exp(jnp.arange(half_width, dtype=jnp.float32) * (-2.0 * math.log(10000.0) / values.shape[-1]))
    angles = position.astype(jnp.float32).reshape(position.shape + (1,) * (values.ndim - 1)) * frequency
    cosine = jnp.cos(angles)
    sine_part = jnp.sin(angles)
    first_half = values[..., :half_width]
    second_half = values[..., half_width:]
    return jnp.concatenate([first_half * cosine - second_half * sine_part, second_half * cosine + first_half * sine_part], axis=-1)

def positions(row_ids, block_ids, rows_dev):
    half_width = rows_dev // 2
    device = row_ids // rows_dev
    within = row_ids % rows_dev
    block_num = block_ids.reshape(-1)[device * 2 + within // half_width]
    return block_num * half_width + within % half_width

def rounded(values):
    return lax.optimization_barrier(values.astype(jnp.bfloat16)).astype(jnp.float32)

def reference(tokens, block_ids, attn_gain, q_weight, kv_weight, kv_gain, uk_weight, uv_weight, o_weight, ffn_gain, w_gate, w_up, w_down, routes, gate_weights):
    total_rows = tokens.shape[0]
    row_ids = jnp.arange(total_rows, dtype=jnp.int32)
    row_pos = positions(row_ids, block_ids, TOK_DEV)
    normed = normalize(tokens, attn_gain).astype(jnp.bfloat16)
    queries = jnp.dot(normed, q_weight, preferred_element_type=jnp.float32).astype(jnp.bfloat16)
    queries = queries.reshape(total_rows, HEADS, NOPE + ROPE)
    query_rope = rounded(rotate(queries[..., NOPE:].astype(jnp.float32), row_pos))
    query_latent = rounded(jnp.einsum('thn,hln->thl', queries[..., :NOPE].astype(jnp.float32), uk_weight.astype(jnp.float32)))
    projected = jnp.dot(normed, kv_weight, preferred_element_type=jnp.float32)
    latent = rounded(normalize(projected[:, :LATENT], kv_gain))
    key_rope = rounded(rotate(projected[:, LATENT:], row_pos))
    block_rows = math.gcd(total_rows, 256)
    score_scale = (NOPE + ROPE) ** (-0.5)

    def attend(block_index):
        first_row = block_index * block_rows
        q_lat = lax.dynamic_slice_in_dim(query_latent, first_row, block_rows, 0)
        q_rot = lax.dynamic_slice_in_dim(query_rope, first_row, block_rows, 0)
        q_pos = lax.dynamic_slice_in_dim(row_pos, first_row, block_rows, 0)
        scores = (jnp.einsum('thl,kl->thk', q_lat, latent) + jnp.einsum('thr,kr->thk', q_rot, key_rope)) * score_scale
        allowed = row_pos[None, None, :] <= q_pos[:, None, None]
        scores = jnp.where(allowed, scores, -1e+30)
        top_score = lax.optimization_barrier(jnp.max(scores, axis=-1, keepdims=True))
        exp_terms = jnp.where(allowed, jnp.exp(scores - top_score), 0.0)
        row_total = lax.optimization_barrier(jnp.sum(exp_terms, axis=-1))
        mixed_latent = jnp.einsum('thk,kl->thl', rounded(exp_terms), latent)
        return (mixed_latent / row_total[..., None]).astype(jnp.bfloat16)
    out_latent = lax.map(attend, jnp.arange(total_rows // block_rows, dtype=jnp.int32))
    out_latent = out_latent.reshape(total_rows, HEADS, LATENT)
    head_out = jnp.einsum('thl,hlv->thv', out_latent.astype(jnp.float32), uv_weight.astype(jnp.float32)).astype(jnp.bfloat16)
    head_out = head_out.reshape(total_rows, HEADS * VDIM)
    mixed = (tokens.astype(jnp.float32) + jnp.dot(head_out, o_weight, preferred_element_type=jnp.float32)).astype(jnp.bfloat16)
    normed_ffn = normalize(mixed, ffn_gain).astype(jnp.bfloat16)
    flat_routes = routes.reshape(-1)
    order_ids = jnp.argsort(flat_routes, stable=True).astype(jnp.int32)
    counts = jax.ops.segment_sum(jnp.ones_like(flat_routes), flat_routes, num_segments=EXPERTS)
    offsets = jnp.cumsum(counts) - counts
    window = DEVICES * CAP
    padded = jnp.concatenate([order_ids, jnp.zeros((window,), jnp.int32)])
    flat_gates = gate_weights.reshape(-1)

    def per_expert(accumulated, inputs):
        expert, gate_w, up_w, down_w = inputs
        picked = lax.dynamic_slice_in_dim(padded, offsets[expert].astype(jnp.int32), window, 0)
        live = jnp.arange(window, dtype=jnp.int32) < counts[expert]
        token_ids = picked // TOPK
        rows_in = normed_ffn[token_ids]
        gate_part = jnp.dot(rows_in, gate_w, preferred_element_type=jnp.float32)
        up_part = jnp.dot(rows_in, up_w, preferred_element_type=jnp.float32)
        hidden = (jax.nn.silu(gate_part) * up_part).astype(jnp.bfloat16)
        expert_out = rounded(jnp.dot(hidden, down_w, preferred_element_type=jnp.float32))
        weight_col = jnp.where(live, flat_gates[picked], 0.0)
        return (accumulated.at[token_ids].add(weight_col[:, None] * expert_out), None)
    combined, unused = lax.scan(per_expert, jnp.zeros((total_rows, D), jnp.float32), (jnp.arange(EXPERTS, dtype=jnp.int32), w_gate, w_up, w_down))
    return (mixed.astype(jnp.float32) + combined).astype(jnp.bfloat16)
```

```python
import math

import jax
import jax.numpy as jnp
from jax import lax
from jax.experimental import pallas as pl
from jax.experimental.pallas import tpu as pltpu
from jax.sharding import PartitionSpec as P

EPSILON = 1e-06


def normalize(values, gain_vec):
    values = values.astype(jnp.float32)
    factor = lax.rsqrt(jnp.mean(values * values, axis=-1, keepdims=True) + EPSILON)
    return values * factor * gain_vec


def rotate(values, position):
    half_width = values.shape[-1] // 2
    frequency = jnp.exp(
        jnp.arange(half_width, dtype=jnp.float32) * (-2.0 * math.log(10000.0) / values.shape[-1])
    )
    angles = (
        position.astype(jnp.float32).reshape(position.shape + (1,) * (values.ndim - 1)) * frequency
    )
    cosine = jnp.cos(angles)
    sine_part = jnp.sin(angles)
    first_half = values[..., :half_width]
    second_half = values[..., half_width:]
    return jnp.concatenate(
        [
            first_half * cosine - second_half * sine_part,
            second_half * cosine + first_half * sine_part,
        ],
        axis=-1,
    )


def positions(row_ids, block_ids, rows_dev):
    half_width = rows_dev // 2
    device = row_ids // rows_dev
    within = row_ids % rows_dev
    block_num = block_ids.reshape(-1)[device * 2 + within // half_width]
    return block_num * half_width + within % half_width


def plain_body(
    tokens,
    block_ids,
    attn_gain,
    q_weight,
    kv_weight,
    kv_gain,
    uk_weight,
    uv_weight,
    o_weight,
    ffn_gain,
    w_gate,
    w_up,
    w_down,
    routes,
    gate_weights,
):
    tp_count = lax.axis_size("tp")
    seq_count = lax.axis_size("seq")
    tp_index = lax.axis_index("tp")
    seq_index = lax.axis_index("seq")
    sub_rows = tokens.shape[0]
    dev_rows = sub_rows * tp_count
    model_dim = tokens.shape[1]
    head_count = uk_weight.shape[0]
    latent_dim = uk_weight.shape[1]
    nope_dim = uk_weight.shape[2]
    rope_dim = kv_weight.shape[1] - latent_dim
    value_dim = uv_weight.shape[2]
    top_count = routes.shape[1]
    capacity = min(sub_rows, max(2, 3 * sub_rows * top_count // (2 * seq_count)))
    score_scale = (nope_dim + rope_dim) ** (-0.5)
    all_tokens = lax.all_gather(tokens, "tp", axis=0, tiled=True)
    normed = normalize(all_tokens, attn_gain).astype(jnp.bfloat16)
    query_ids = seq_index * dev_rows + jnp.arange(dev_rows, dtype=jnp.int32)
    query_pos = positions(query_ids, block_ids, dev_rows)
    queries = jnp.dot(normed, q_weight, preferred_element_type=jnp.float32).astype(jnp.bfloat16)
    queries = queries.reshape(dev_rows, head_count, nope_dim + rope_dim)
    query_rope = rotate(queries[..., nope_dim:].astype(jnp.float32), query_pos).astype(jnp.bfloat16)
    query_latent = jnp.einsum(
        "thn,hln->thl", queries[..., :nope_dim], uk_weight, preferred_element_type=jnp.float32
    ).astype(jnp.bfloat16)
    projected = jnp.dot(normed, kv_weight, preferred_element_type=jnp.float32)
    latent = normalize(projected[:, :latent_dim], kv_gain).astype(jnp.bfloat16)
    key_rope = rotate(projected[:, latent_dim:], query_pos).astype(jnp.bfloat16)
    latent, key_rope = (latent, key_rope)
    run_max = jnp.full((dev_rows, head_count), -1e30, jnp.float32)
    piece_latent = lax.all_gather(latent, "seq", axis=0, tiled=True)
    piece_rope = lax.all_gather(key_rope, "seq", axis=0, tiled=True)
    count_rows = piece_latent.shape[0]
    key_pos = positions(jnp.arange(count_rows, dtype=jnp.int32), block_ids, dev_rows)
    scores = jnp.einsum(
        "thl,kl->thk", query_latent, piece_latent, preferred_element_type=jnp.float32
    )
    scores = scores + jnp.einsum(
        "thr,kr->thk", query_rope, piece_rope, preferred_element_type=jnp.float32
    )
    scores = scores * score_scale
    allowed = key_pos[None, None, :] <= query_pos[:, None, None]
    scores = jnp.where(allowed, scores, -1e30)
    new_max = jnp.maximum(run_max, jnp.max(scores, axis=-1))
    exp_terms = jnp.where(allowed, jnp.exp(scores - new_max[..., None]), 0.0)
    run_sum = jnp.sum(exp_terms, axis=-1)
    accumulated = jnp.einsum(
        "thk,kl->thl",
        exp_terms.astype(jnp.bfloat16),
        piece_latent,
        preferred_element_type=jnp.float32,
    )
    folded = (new_max, run_sum, accumulated)
    run_max, run_sum, accumulated = folded
    out_latent = (accumulated / run_sum[..., None]).astype(jnp.bfloat16)
    head_out = jnp.einsum(
        "thl,hlv->thv", out_latent, uv_weight, preferred_element_type=jnp.float32
    ).astype(jnp.bfloat16)
    partial_out = jnp.dot(
        head_out.reshape(dev_rows, head_count * value_dim),
        o_weight,
        preferred_element_type=jnp.float32,
    )
    expert_ids = jnp.arange(seq_count, dtype=jnp.int32)

    def slot_table(route_rows):
        flat_ids = route_rows.reshape(-1)
        onehot = (flat_ids[:, None] == expert_ids[None, :]).astype(jnp.int32)
        rank_table = jnp.cumsum(onehot, axis=0) - onehot
        return flat_ids * capacity + jnp.sum(rank_table * onehot, axis=1)

    own_routes = lax.dynamic_slice_in_dim(routes, tp_index * sub_rows, sub_rows, 0)
    own_weights = lax.dynamic_slice_in_dim(gate_weights, tp_index * sub_rows, sub_rows, 0)
    attn_own = lax.psum_scatter(
        partial_out.astype(jnp.bfloat16), "tp", scatter_dimension=0, tiled=True
    ).astype(jnp.float32)
    mixed_rows = (tokens.astype(jnp.float32) + attn_own).astype(jnp.bfloat16)
    normed_own = normalize(mixed_rows, ffn_gain).astype(jnp.bfloat16)
    target = slot_table(own_routes)
    source = jnp.arange(target.shape[0], dtype=jnp.int32) // top_count
    buffer = (
        jnp.zeros((seq_count * capacity, model_dim), jnp.bfloat16)
        .at[target]
        .set(normed_own[source])
    )
    packed = buffer.reshape(seq_count, capacity, model_dim)
    arrived = lax.all_to_all(packed, "seq", split_axis=0, concat_axis=0, tiled=True)
    piece_data = lax.all_gather(arrived, "tp", axis=0, tiled=True)
    flat_rows = piece_data.reshape(-1, model_dim)
    gate_part = jnp.dot(flat_rows, w_gate[0], preferred_element_type=jnp.float32)
    up_part = jnp.dot(flat_rows, w_up[0], preferred_element_type=jnp.float32)
    hidden = (
        (jax.nn.silu(gate_part) * up_part)
        .astype(jnp.bfloat16)
        .reshape(piece_data.shape[0], capacity, -1)
        .reshape(-1, w_up.shape[2])
    )
    down_local = w_down[0]
    expert_out = lax.psum_scatter(
        jnp.dot(hidden, down_local, preferred_element_type=jnp.float32).astype(jnp.bfloat16),
        "tp",
        scatter_dimension=0,
        tiled=True,
    ).astype(jnp.float32)
    expert_out = expert_out.astype(jnp.bfloat16).reshape(seq_count, capacity, model_dim)
    returned = lax.all_to_all(expert_out, "seq", split_axis=0, concat_axis=0, tiled=True).reshape(
        seq_count * capacity, model_dim
    )
    picked = (
        returned[slot_table(own_routes)].astype(jnp.float32).reshape(sub_rows, top_count, model_dim)
    )
    combined = jnp.sum(picked * own_weights[..., None], axis=1)
    return (mixed_rows.astype(jnp.float32) + combined).astype(jnp.bfloat16)


PLANE = 4
GROUPS = ((0,), (1, 3), (2,))
F32 = jnp.float32
BF16 = jnp.bfloat16


def params(megabytes):
    return pltpu.CompilerParams(vmem_limit_bytes=megabytes * 1024 * 1024)


def cost(flops, bytes_accessed, transcendentals=0):
    return pl.CostEstimate(
        flops=int(flops), bytes_accessed=int(bytes_accessed), transcendentals=int(transcendentals)
    )


def vmem():
    return pl.BlockSpec(memory_space=pltpu.VMEM)


def smem():
    return pl.BlockSpec(memory_space=pltpu.SMEM)


def anywhere():
    return pl.BlockSpec(memory_space=pl.ANY)


def shape(rows, columns, dtype):
    return jax.ShapeDtypeStruct((rows, columns), dtype)


def tiles(extent, step):
    return [(first, min(first + step, extent)) for first in range(0, extent, step)]


def whole_tiles(rows):
    return -(-rows // 16) * 16


def swap_halves(values):
    half = values.shape[-1] // 2
    return jnp.concatenate([values[:, half:], values[:, :half]], axis=1)


def dot_nt(left, right):
    return lax.dot_general(left, right, (((1,), (1,)), ((), ())), preferred_element_type=F32)


def dot(left, right):
    return jnp.dot(left, right, preferred_element_type=F32)


def latent_kernel(
    block_ids, tokens, gain, weight, kv_gain, routes, gates, out, cosine, sine
):
    rows = tokens.shape[0]
    latent_dim = kv_gain.shape[1]
    rope_dim = cosine.shape[1]
    core = lax.axis_index("tp")
    place = lax.axis_index("seq")
    row = lax.broadcasted_iota(jnp.int32, (2 * rows, 1), 0)
    block = jnp.where(row < rows, block_ids[0, place], block_ids[1, place])
    pos = (block * rows + row % rows).astype(F32)
    lane = lax.broadcasted_iota(jnp.int32, (1, rope_dim // 2), 1).astype(F32)
    angles = pos * jnp.exp(lane * (-2.0 * math.log(10000.0) / rope_dim))
    cos_part, sin_part = jnp.cos(angles), jnp.sin(angles)
    cosine[...] = jnp.concatenate([cos_part, cos_part], axis=1)
    sine[...] = jnp.concatenate([-sin_part, sin_part], axis=1)

    normed = normalize(tokens[...], gain[...]).astype(BF16)
    projected = dot_nt(normed, weight[...])
    latent = normalize(projected[:, :latent_dim], kv_gain[...])
    rope = projected[:, latent_dim:]
    own = pl.ds(pl.multiple_of(core * rows, rows), rows)
    rope = rope * cosine[own, :] + swap_halves(rope) * sine[own, :]

    gate = gates[...]
    first = gate.astype(BF16)
    rest = gate - first.astype(F32)
    second = rest.astype(BF16)
    third = (rest - second.astype(F32)).astype(BF16)
    info = jnp.concatenate(
        [routes[...].astype(F32)] + [part.astype(F32) for part in (first, second, third)], axis=0
    ).astype(BF16)
    at_row = lax.broadcasted_iota(jnp.int32, (rows, 2 * rows), 0)
    at_col = lax.broadcasted_iota(jnp.int32, (rows, 2 * rows), 1)
    info = dot_nt((at_col == at_row + core * rows).astype(BF16), info)
    spare = out.shape[1] - latent_dim - rope_dim - info.shape[1]
    out[:, :latent_dim] = latent.astype(BF16)
    out[:, latent_dim:] = jnp.concatenate(
        [rope, info, jnp.zeros((rows, spare), F32)], axis=1
    ).astype(BF16)


def query_kernel(own, other, gain, cosine, sine, q_weight, uk_weight, low, high, normed):
    rows = own.shape[0]
    heads, latent_dim, nope = uk_weight.shape
    rope_dim = cosine.shape[1]

    @pl.when(pl.program_id(0) == 0)
    def _():
        core = lax.axis_index("tp")
        normed[pl.ds(pl.multiple_of(core * rows, rows), rows), :] = normalize(
            own[...], gain[...]
        ).astype(BF16)
        normed[pl.ds(pl.multiple_of((1 - core) * rows, rows), rows), :] = normalize(
            other[...], gain[...]
        ).astype(BF16)

    queries = dot(normed[...], q_weight[...]).astype(BF16)
    for head in range(heads):
        first = head * (nope + rope_dim)
        latent = dot_nt(queries[:, first : first + nope], uk_weight[head]).astype(BF16)
        rope = queries[:, first + nope : first + nope + rope_dim].astype(F32)
        rope = rope * cosine[...] + swap_halves(rope) * sine[...]
        rope = jnp.concatenate([rope, jnp.zeros_like(rope)], axis=1).astype(BF16)
        here = slice(head * rows, (head + 1) * rows)
        low[here, :latent_dim] = latent[:rows]
        low[here, latent_dim:] = rope[:rows]
        high[here, :latent_dim] = latent[rows:]
        high[here, latent_dim:] = rope[rows:]


def attention_kernel(scale, order, pieces, *refs):
    block_ids, low, high = refs[:3]
    piece_refs = refs[3 : 3 + 2 * pieces]
    uv_hbm, o_hbm, keep, send = refs[3 + 2 * pieces : 7 + 2 * pieces]
    keys, uv, o, out_low, out_high, head_out, total, key_sems, w_sems = refs[7 + 2 * pieces :]
    me = lax.axis_index("tp")
    place = lax.axis_index("seq")
    copies = []
    first = 0
    for i, piece in enumerate(piece_refs):
        side = me if i < pieces else 1 - me
        first = 0 if i == pieces else first
        size = piece.shape[0]
        copies.append(
            pltpu.make_async_copy(piece, keys.at[side, pl.ds(first, size)], key_sems.at[i])
        )
        first += size
    uv_copy = pltpu.make_async_copy(uv_hbm, uv, w_sems.at[0])
    o_copy = pltpu.make_async_copy(o_hbm, o, w_sems.at[1])
    for copy in copies:
        copy.start()
    uv_copy.start()
    o_copy.start()
    heads, latent_dim, value_dim = uv.shape
    query_rows = low.shape[0]
    rows = query_rows // heads
    layers = block_ids.shape[1] // PLANE
    key_lane = lax.broadcasted_iota(jnp.int32, (1, len(order) * rows), 1)
    key_block = [jnp.zeros_like(key_lane), jnp.zeros_like(key_lane)]
    layer, inner = place // PLANE, place % PLANE
    for i, (j, k) in enumerate(order):
        source = lax.rem(layer + layers - k, layers) * PLANE + (inner ^ j)
        for side in range(2):
            key_block[side] = jnp.where(
                key_lane // rows == i, block_ids[side, source], key_block[side]
            )
    for copy in copies:
        copy.wait()
    tile = min(256, query_rows)
    within = lax.broadcasted_iota(jnp.int32, (tile, 1), 0) % rows
    for first in range(0, query_rows, tile):
        here = slice(first, first + tile)
        for queries, side, out in ((low, 0, out_low), (high, 1, out_high)):
            q = queries[here, :]
            key_pos = key_block[side] * rows + key_lane % rows
            allowed = key_pos <= block_ids[side, place] * rows + within
            masked = jnp.where(allowed, dot_nt(q, keys[side]), -1e30)
            top = jnp.max(masked, axis=1, keepdims=True)
            if side == 1:
                plain = dot_nt(q, keys[0])
                top = jnp.maximum(top, jnp.max(plain, axis=1, keepdims=True))
            terms = jnp.exp((masked - top) * scale)
            row_sum = jnp.sum(terms, axis=1, keepdims=True)
            mixed = dot(terms.astype(BF16), keys[side, :, :latent_dim])
            if side == 1:
                terms = jnp.exp((plain - top) * scale)
                row_sum = row_sum + jnp.sum(terms, axis=1, keepdims=True)
                mixed = mixed + dot(terms.astype(BF16), keys[0, :, :latent_dim])
            out[here, :] = (mixed / row_sum).astype(BF16)
    uv_copy.wait()
    for head in range(heads):
        here = slice(head * rows, (head + 1) * rows)
        both = jnp.concatenate([out_low[here, :], out_high[here, :]], axis=0)
        head_out[:, head * value_dim : (head + 1) * value_dim] = dot(both, uv[head]).astype(BF16)
    o_copy.wait()
    for first, last in tiles(o.shape[1], 512):
        total[:, first:last] = dot(head_out[...], o[:, first:last])
    keep[...] = total[pl.ds(pl.multiple_of(me * rows, rows), rows), :]
    send[...] = total[pl.ds(pl.multiple_of((1 - me) * rows, rows), rows), :].astype(BF16)


def mixed_kernel(tokens, keep, received, gain, mixed, normed):
    attn = keep[...] + received[...].astype(F32)
    rounded = (tokens[...].astype(F32) + attn).astype(BF16)
    mixed[...] = rounded
    normed[...] = normalize(rounded, gain[...]).astype(BF16)


def table_kernel(capacity, rows, top, info_at, *refs):
    blocks = refs[0]
    slot_rows, slot_cols, gate_cols = (refs[1 + i :: 3] for i in range(3))
    dests = slot_rows[0].shape[0]
    place = lax.axis_index("seq")
    at_row = lax.broadcasted_iota(jnp.int32, (rows, rows), 0)
    at_col = lax.broadcasted_iota(jnp.int32, (rows, rows), 1)
    before = (at_col < at_row).astype(BF16)
    same = (at_col == at_row).astype(BF16)
    lane = lax.broadcasted_iota(jnp.int32, (rows, dests), 1)
    for g, group in enumerate(GROUPS):
        for i, k in enumerate(group):
            block = blocks[k * rows : (k + 1) * rows, info_at:].astype(F32)
            routes = block[:, :top]
            gates = block[:, top : 2 * top] + block[:, 2 * top : 3 * top]
            gates = gates + block[:, 3 * top : 4 * top]
            named = jnp.zeros((rows, dests), F32)
            gate = jnp.zeros((rows, dests), F32)
            for j in range(dests):
                expert = place // PLANE * PLANE + (place % PLANE ^ j)
                hit = (routes == expert.astype(F32)).astype(F32)
                named = jnp.where(lane == j, jnp.sum(hit, axis=1, keepdims=True), named)
                gate = jnp.where(lane == j, jnp.sum(hit * gates, axis=1, keepdims=True), gate)
            rank = dot(before, named.astype(BF16))
            slot = jnp.where(named > 0.5, rank + float(i * capacity), -1.0)
            here = slice(i * rows, (i + 1) * rows)
            slot_cols[g][here, :] = slot
            gate_cols[g][here, :] = gate
            slot_rows[g][:, here] = lax.dot_general(
                slot.astype(BF16), same, (((0,), (0,)), ((), ())), preferred_element_type=F32
            )


def pack_kernel(*refs):
    dests = refs[0].shape[0]
    slot_rows, blocks, outs = refs[0], refs[1:-dests], refs[-dests:]
    packed = outs[0].shape[0]
    stride = whole_tiles(packed)
    values = [block[...] for block in blocks]
    if len(values) * values[0].shape[0] > slot_rows.shape[1]:
        from_below = lax.axis_index("seq") // PLANE >= 2
        values = [jnp.where(from_below, values[0], values[1])]
    values = jnp.concatenate(values, axis=0)
    place = lax.broadcasted_iota(jnp.int32, (stride, values.shape[0]), 0).astype(F32)
    picks = [(place == slot_rows[j : j + 1, :]).astype(BF16) for j in range(dests)]
    picked = dot(jnp.concatenate(picks, axis=0), values).astype(BF16)
    for j, out in enumerate(outs):
        out[...] = picked[j * stride : j * stride + packed, :]


def expert_kernel(*refs):
    rows_got, weights, outs = refs[:PLANE], refs[PLANE : PLANE + 6], refs[PLANE + 6 : 2 * PLANE + 6]
    staged, gate_w, up_w, down_w, sems = refs[2 * PLANE + 6 :]
    copies = []
    for half in range(2):
        for kind, held in enumerate((gate_w, up_w, down_w)):
            copies.append(
                pltpu.make_async_copy(
                    weights[3 * half + kind].at[0], held.at[half], sems.at[half, kind]
                )
            )
    for i in (0, 1, 3, 4, 2, 5):
        copies[i].start()
    packed = rows_got[0].shape[0]
    for j, piece in enumerate(rows_got):
        staged[j * packed : (j + 1) * packed, :] = piece[...].astype(F32)
    rows_in = staged[...].astype(BF16)
    hidden = []
    for half in range(2):
        copies[3 * half].wait()
        gate = dot_nt(rows_in, gate_w[half])
        copies[3 * half + 1].wait()
        up = dot_nt(rows_in, up_w[half])
        hidden.append((gate / (1.0 + jnp.exp(-gate)) * up).astype(BF16))
    copies[2].wait()
    value = dot(hidden[0], down_w[0])
    copies[5].wait()
    staged[...] = value + dot(hidden[1], down_w[1])
    for j, out in enumerate(outs):
        out[...] = staged[j * packed : (j + 1) * packed, :].astype(BF16)


def unpack_kernel(slot_cols, gate_cols, *refs):
    dests = slot_cols.shape[1]
    values, outs = refs[:dests], refs[dests:]
    packed = values[0].shape[0]
    rows = outs[0].shape[0]
    place = lax.broadcasted_iota(jnp.int32, (slot_cols.shape[0], packed), 1).astype(F32)
    total = None
    for j, value in enumerate(values):
        pick = (place == slot_cols[:, j : j + 1]).astype(BF16)
        term = dot(pick, value[...]) * gate_cols[:, j : j + 1]
        total = term if total is None else total + term
    for i, out in enumerate(outs):
        out[...] = total[i * rows : (i + 1) * rows].astype(out.dtype)


def final_kernel(mixed, own, *refs):
    total = own[...]
    for ref in refs[:-1]:
        total = total + ref[...].astype(F32)
    refs[-1][...] = (mixed[...].astype(F32) + total).astype(BF16)


def fast_body(
    tokens,
    block_ids,
    attn_gain,
    q_weight,
    kv_weight,
    kv_gain,
    uk_weight,
    uv_weight,
    o_weight,
    ffn_gain,
    w_gate,
    w_up,
    w_down,
    routes,
    gate_weights,
):
    seq_count = lax.axis_size("seq")
    layers = seq_count // PLANE
    rows, model_dim = tokens.shape
    heads, latent_dim, nope_dim = uk_weight.shape
    rope_dim = kv_weight.shape[1] - latent_dim
    value_dim = uv_weight.shape[2]
    top_count = routes.shape[1]
    units = w_gate.shape[2]
    capacity = min(rows, max(2, 3 * rows * top_count // (2 * seq_count)))
    key_width = latent_dim + 2 * rope_dim
    scale = (nope_dim + rope_dim) ** (-0.5)
    barrier = lax.optimization_barrier

    def along(values, step):
        pairs = [
            (s, ((s // PLANE + step) % layers) * PLANE + s % PLANE) for s in range(seq_count)
        ]
        return lax.ppermute(values, "seq", pairs)

    def forward(values, step):
        pairs = [
            (s, s + step * PLANE)
            for s in range(seq_count)
            if 0 < s // PLANE < layers - 1
        ]
        return lax.ppermute(values, "seq", pairs)

    def across(values, j):
        return lax.ppermute(values, "seq", [(s, s ^ j) for s in range(seq_count)])

    def swap(values):
        return lax.ppermute(values, "tp", [(0, 1), (1, 0)])

    def call(kernel, name, megabytes, flops, bytes_accessed, **options):
        return pl.pallas_call(
            kernel,
            compiler_params=params(megabytes),
            cost_estimate=cost(flops, bytes_accessed),
            name=name,
            **options,
        )

    attn_gain = attn_gain.reshape(1, model_dim)
    kv_gain = kv_gain.reshape(1, latent_dim)
    ffn_gain = ffn_gain.reshape(1, model_dim)

    other_tokens = swap(tokens)
    gate_t, up_t = jnp.swapaxes(w_gate, 1, 2), jnp.swapaxes(w_up, 1, 2)
    gate_other, up_other = swap(gate_t), swap(up_t)

    latents, cosine, sine = call(
        latent_kernel,
        "own_latents",
        56,
        2 * rows * model_dim * key_width,
        kv_weight.size * 2,
        out_shape=(
            shape(rows, key_width, BF16),
            shape(2 * rows, rope_dim, F32),
            shape(2 * rows, rope_dim, F32),
        ),
        in_specs=[smem()] + [vmem()] * 6,
        out_specs=(vmem(),) * 3,
    )(block_ids.T, tokens, attn_gain, kv_weight.T, kv_gain, routes.T, gate_weights.T)

    column_keys = jnp.concatenate(
        [latents] + [along(latents, k) for k in range(1, layers)], axis=0
    )
    far = [across(column_keys, j) for j in range(1, PLANE)]
    other_tokens, cosine, sine, behind = barrier((other_tokens, cosine, sine, column_keys))

    pair = 2
    low, high = call(
        query_kernel,
        "queries",
        20,
        4 * rows * (q_weight.size + uk_weight.size),
        2 * (q_weight.size + uk_weight.size),
        grid=(heads // pair,),
        out_shape=(shape(heads * rows, key_width, BF16),) * 2,
        in_specs=[vmem()] * 5
        + [
            pl.BlockSpec((model_dim, pair * (nope_dim + rope_dim)), lambda i: (0, i)),
            pl.BlockSpec((pair, latent_dim, nope_dim), lambda i: (i, 0, 0)),
        ],
        out_specs=(pl.BlockSpec((pair * rows, key_width), lambda i: (i, 0)),) * 2,
        scratch_shapes=[pltpu.VMEM((2 * rows, model_dim), BF16)],
    )(tokens, other_tokens, attn_gain, cosine, sine, q_weight, uk_weight)

    column = layers * rows
    slots = call(
        lambda *refs: table_kernel(capacity, rows, top_count, latent_dim + rope_dim, *refs),
        "row_tables",
        8,
        column * rows * 8,
        column * 128 * 12,
        out_shape=tuple(
            part
            for group in GROUPS
            for part in (
                shape(PLANE, len(group) * rows, F32),
                shape(len(group) * rows, PLANE, F32),
                shape(len(group) * rows, PLANE, F32),
            )
        ),
        in_specs=[vmem()],
        out_specs=(vmem(),) * (3 * len(GROUPS)),
    )(behind)
    far, low, high, slots, gate_other = barrier((far, low, high, slots, gate_other))
    own_keys = [column_keys] + far
    other_keys = [swap(piece) for piece in own_keys]
    order = [(j, k) for j in range(PLANE) for k in range(layers)]

    *other_keys, ready = barrier((*other_keys, w_down))
    down_other = swap(ready)

    keep, send = call(
        lambda *refs: attention_kernel(scale, order, len(own_keys), *refs),
        "attention",
        28,
        3 * 2 * heads * rows * seq_count * rows * (key_width + latent_dim),
        2 * (o_weight.size + uv_weight.size),
        out_shape=(shape(rows, model_dim, F32), shape(rows, model_dim, BF16)),
        in_specs=[smem(), vmem(), vmem()] + [anywhere()] * (2 * len(own_keys) + 2),
        out_specs=(vmem(), vmem()),
        scratch_shapes=[
            pltpu.VMEM((2, seq_count * rows, key_width), BF16),
            pltpu.VMEM(uv_weight.shape, BF16),
            pltpu.VMEM(o_weight.shape, BF16),
            pltpu.VMEM((heads * rows, latent_dim), BF16),
            pltpu.VMEM((heads * rows, latent_dim), BF16),
            pltpu.VMEM((2 * rows, heads * value_dim), BF16),
            pltpu.VMEM((2 * rows, model_dim), F32),
            pltpu.SemaphoreType.DMA((2 * len(own_keys),)),
            pltpu.SemaphoreType.DMA((2,)),
        ],
    )(block_ids.T, low, high, *own_keys, *other_keys, uv_weight, o_weight)
    received, gate_other, up_other, down_other = barrier(
        (swap(send), gate_other, up_other, down_other)
    )

    mixed, normed = call(
        mixed_kernel,
        "mixed_rows",
        8,
        rows * model_dim * 8,
        rows * model_dim * 12,
        out_shape=(shape(rows, model_dim, BF16),) * 2,
        in_specs=[vmem()] * 4,
        out_specs=(vmem(),) * 2,
    )(tokens, keep, received, ffn_gain)

    def expert(got):
        packed = got[0].shape[0]
        return call(
            expert_kernel,
            "expert",
            40,
            0,
            0,
            out_shape=(shape(packed, model_dim, BF16),) * PLANE,
            in_specs=[vmem()] * PLANE + [anywhere()] * 6,
            out_specs=(vmem(),) * PLANE,
            scratch_shapes=[
                pltpu.VMEM((PLANE * packed, model_dim), F32),
                pltpu.VMEM((2,) + gate_t.shape[1:], BF16),
                pltpu.VMEM((2,) + gate_t.shape[1:], BF16),
                pltpu.VMEM((2,) + w_down.shape[1:], BF16),
                pltpu.SemaphoreType.DMA((2, 3)),
            ],
        )(*got, gate_t, up_t, w_down, gate_other, up_other, down_other)

    beside = {k: along(normed, k) for k in (1, layers - 1)}
    arrivals = [[normed], list(beside.values()), []]
    pieces = []
    for g, group in enumerate(GROUPS):
        packed = len(group) * capacity
        if g == 2:
            above, below, *_ = barrier((beside[1], beside[layers - 1], *pieces[0]))
            arrivals[2] = [forward(above, 1), forward(below, -1)]
            expert_outs = [expert(pieces[0])]
            arrivals[2], *_ = barrier((arrivals[2], *expert_outs[0]))
        outs = call(
            pack_kernel,
            "pack_rows",
            12,
            0,
            0,
            out_shape=(shape(packed, model_dim, BF16),) * PLANE,
            in_specs=[vmem()] * (1 + len(arrivals[g])),
            out_specs=(vmem(),) * PLANE,
        )(slots[3 * g], *arrivals[g])
        if g == 1:
            own, *outs = barrier((pieces[0][0], *outs))
            pieces[0][0] = own
        pieces.append([outs[0]] + [across(outs[j], j) for j in range(1, PLANE)])

    for got in pieces[1:]:
        got, *_ = barrier((got, *expert_outs[-1]))
        expert_outs.append(expert(got))

    sums, done = [None] * layers, []
    for g in (1, 2, 0):
        group, outs = GROUPS[g], expert_outs[g]
        if g == 1:
            outs, *_ = barrier((list(outs), *pieces[2]))
        if g == 0:
            outs, *_ = barrier((list(outs), *done, sums[1], sums[layers - 1]))
        returned = [across(outs[j], j) for j in range(1, PLANE)]
        if g == 1:
            returned, *_ = barrier((returned, *expert_outs[2]))
        results = call(
            unpack_kernel,
            "unpack_rows",
            12,
            0,
            0,
            out_shape=tuple(shape(rows, model_dim, BF16 if k else F32) for k in group),
            in_specs=[vmem()] * (2 + PLANE),
            out_specs=(vmem(),) * len(group),
        )(
            slots[3 * g + 1],
            slots[3 * g + 2],
            outs[0],
            *returned,
        )
        done += results
        for k, result in zip(group, results):
            sums[k] = along(result, -k) if k else result

    return call(
        final_kernel,
        "layer_out",
        8,
        rows * model_dim * 8,
        rows * model_dim * 14,
        out_shape=shape(rows, model_dim, BF16),
        in_specs=[vmem()] * (1 + layers),
        out_specs=vmem(),
    )(mixed, *sums)


def solution(mesh):
    fits = mesh.shape["tp"] == 2 and mesh.shape["seq"] == 4 * PLANE
    return jax.shard_map(
        fast_body if fits else plain_body,
        mesh=mesh,
        in_specs=(
            P(("seq", "tp"), None),
            P(),
            P(),
            P(None, "tp"),
            P(),
            P(),
            P("tp", None, None),
            P("tp", None, None),
            P("tp", None),
            P(),
            P("seq", None, "tp"),
            P("seq", None, "tp"),
            P("seq", "tp", None),
            P("seq", None),
            P("seq", None),
        ),
        out_specs=P(("seq", "tp"), None),
        check_vma=False,
    )
```
